512 devices in a mesh: row: 64 (over y, z_hi, core), col: 8 (over x, z_lo).
Axes of the slice: x: 4, y: 8, z: 8 (z_hi: 4, z_lo: 2; z = z_hi * 2 + z_lo), core: 2. Of those that a mesh axis runs over, the one named last changes fastest.
Arguments:
- panel_u: bfloat16 [64, 128, 2688], P('row', None, 'col'), may hold values from -0.115727512 to 0.115727512
- panel_v: bfloat16 [64, 128, 2688], P('row', None, 'col'), may hold values from -0.07324219 to 0.07324219
- panel_rank: int32 [64], P('row'), may hold values from 1 to 128
- trail_x: bfloat16 [512, 128, 2688], P('row', None, 'col'), may hold values from -6 to 6
- trail_y: bfloat16 [512, 128, 2688], P('row', None, 'col'), may hold values from -6 to 6
- trail_rank: int32 [512], P('row'), may hold values from 1 to 128
- tile_cols: int32 [512], P('row'), may hold values from 0 to 63
- owner: int32 [512, 1], P('row'), may hold values from 0 to 7; in each aligned block of 8 rows (0 to 7, 8 to 15, ...) at most 2 rows name the same one
Outputs:
- left_own: float32 [1024, 128, 128], P(('row', 'col'))
- left_cross: float32 [1024, 128, 128], P(('row', 'col'))
- left_new: float32 [1024, 128, 128], P(('row', 'col'))
- right_own: float32 [1024, 128, 128], P(('row', 'col'))
- right_cross: float32 [1024, 128, 128], P(('row', 'col'))
The draws below stay inside these ranges and needn't reach their ends.
Inputs may be any that keep to these rules, and one draw needn't show every extreme that they name: Among the 8 trailing tiles of one grid row no owner holds more than 2.
All inputs are finite; a program needn't handle non-finite values.
Results may differ from the reference program's by a relative error of at most 0.0003.
Values may be sent and summed in bfloat16 or wider, within the bound.
No kernel may reach another device: no remote copies, remote signals or barrier semaphores. Data moves between devices by JAX's collectives and lax.ppermute only.
A program may use at most 128 MiB of HBM per device.

```python
import math
import jax
import jax.numpy as jnp
import numpy as np
from jax import lax

NB = 2688
KMAX = 128
TT = 8
NP = 64
NT = 512
CAP = 2
SLOTS = 1024
N_ROW = 64
N_COL = 8


def draw_panel_u(key, part):
    key = jax.random.fold_in(key, 11)
    noise_key, common_key = jax.random.split(key)
    noise = jax.random.normal(noise_key, (NP, KMAX, NB), jnp.float32)
    common = 0.6 * jax.random.normal(common_key, (NP, 1, NB), jnp.float32)
    total = jnp.clip(noise + common, -6.0, 6.0)
    return (total * NB ** (-0.5)).astype(jnp.bfloat16)


def draw_panel_rank(key, part):
    key = jax.random.fold_in(key, 12)
    values = jax.random.randint(key, (NP,), 1, KMAX + 1)
    return values.at[0].set(KMAX).at[1].set(1).astype(jnp.int32)


def draw_trail_rank(key, part):
    key = jax.random.fold_in(key, 13)
    values = jax.random.randint(key, (NT,), 1, KMAX + 1)
    return values.at[0].set(KMAX).at[1].set(1).astype(jnp.int32)


def touch_ends(entries, rng, low, top_value):
    shape = entries.shape
    spot = [jax.random.randint(jax.random.fold_in(rng, axis), (), 0, shape[axis]) for axis in range(len(shape))]
    entries = entries.at[tuple(spot)].set(low)
    longest = shape.index(max(shape))
    spot[longest] = (spot[longest] + 1) % shape[longest]
    return entries.at[tuple(spot)].set(top_value)


def block_levels(own_key, dims, shards, smallest, largest):
    gain = 1.0
    for axis_at, parts in shards:
        heights = jax.random.uniform(jax.random.fold_in(jax.random.fold_in(own_key, 6), axis_at), (parts,), jnp.float32, smallest / len(shards), largest / len(shards))
        gain = gain * jnp.repeat(jnp.exp(heights), dims[axis_at] // parts).reshape((-1,) + (1,) * (len(dims) - 1 - axis_at))
    return gain


def assign_block(own_key, own, number, rows, count, top, most, slope):
    sequence = jax.random.permutation(own_key, count)
    heavy_load, ordinary = portions_of(count, rows * top, most, slope, True), portions_of(count, rows * top, most, slope, False)
    places = jnp.arange(count)

    def named(sizes, turn):
        used = int((sizes > 0).sum())
        fixed = max(1, used // 4)
        passed = fixed + (places - fixed + turn * (used - fixed)) % max(1, count - fixed)
        return jnp.zeros((count,), jnp.int32).at[sequence[jnp.where(places < fixed, places, passed)]].set(jnp.asarray(sizes, jnp.int32))

    sizes = jnp.where(number % 4 == 0, named(heavy_load, number // 4), named(ordinary, number - number // 4 - 1))
    mixed = jax.random.permutation(jax.random.fold_in(own, 3), count)
    donor, sink = mixed[0:count // 2 * 2:2], mixed[1:count // 2 * 2:2]
    room = jnp.minimum(sizes[donor] - 1, most - sizes[sink]) // 2
    room = jnp.where((donor == sequence[0]) | (sink == sequence[0]) | (sizes[sink] == 0), 0, jnp.maximum(room, 0))
    passed = jax.random.randint(jax.random.fold_in(own, 4), (count // 2,), 0, 1 << 20) % (room + 1)
    sizes = sizes.at[donor].add(-passed).at[sink].add(passed)
    items = jnp.searchsorted(jnp.cumsum(sizes), jnp.arange(rows * top), side="right").astype(jnp.int32)
    table = items.reshape(top, rows).T
    table = table[jax.random.permutation(jax.random.fold_in(own, 1), rows)]
    turn = jax.random.randint(jax.random.fold_in(own, 2), (rows, 1), 0, top)
    return jnp.take_along_axis(table, (jnp.arange(top)[None, :] + turn) % top, axis=1)


def portions_of(amount, total, most, lean, full):
    portions = [(1 << 20) // math.isqrt(rank ** lean) + 1 for rank in range(1, amount + 1)]
    largest = most if full else min(most, max(-(-total // amount), total * portions[0] // sum(portions)))
    least = 1 if total - largest >= amount - 1 else 0
    holding, spare = [largest] + [least] * (amount - 1), total - largest - least * (amount - 1)
    while spare > 0:
        movable = [i for i in range(1, amount) if holding[i] < largest] or [i for i in range(1, amount) if holding[i] < most]
        mass, budget = sum([portions[i] for i in movable]), spare
        for i in movable:
            extra = min(most - holding[i], max(1, budget * portions[i] // mass), spare)
            holding[i] = holding[i] + extra
            spare = spare - extra
    return np.array(holding)


def bell_draw(rng, extent, spread, most, pieces=(), kind=jnp.bfloat16):
    loudness = block_levels(rng, extent, pieces, -0.22, 0.18) if pieces else 1.0
    entries = jax.random.normal(rng, extent, jnp.float32) * spread * loudness
    return jnp.minimum(jnp.maximum(entries, -most), most).astype(kind)


def setup_inputs(seed: int = 0) -> dict:
    seeds = jax.random.split(jax.random.key(seed), 9)
    panel_u = draw_panel_u(jax.random.fold_in(seeds[8], 71), 0)
    panel_v = bell_draw(seeds[1], (NP, KMAX, NB), (KMAX ** -0.5 * NB ** -0.25), 0.07324219, ((0, 64), (2, 8)))
    panel_rank = draw_panel_rank(jax.random.fold_in(seeds[8], 71), 0)
    trail_x = bell_draw(seeds[3], (NT, KMAX, NB), 1.0, 6.0, ((0, 64), (2, 8)))
    trail_y = bell_draw(seeds[4], (NT, KMAX, NB), 1.0, 6.0, ((0, 64), (2, 8)))
    trail_rank = draw_trail_rank(jax.random.fold_in(seeds[8], 71), 0)
    tile_cols = touch_ends(jax.random.randint(seeds[6], (NT,), 0, NP), jax.random.fold_in(seeds[6], 1), 0, NP - 1).astype(jnp.int32)
    owner_keys = jax.random.split(jax.random.fold_in(seeds[7], 1), NT // TT)
    owner_turns = jax.random.permutation(jax.random.fold_in(seeds[7], 3), NT // TT)
    owner = jax.vmap(lambda own, number: assign_block(jax.random.fold_in(seeds[7], 2), own, number, TT, N_COL, 1, CAP, 2))(owner_keys, owner_turns).reshape((NT, 1))
    return dict(panel_u=panel_u, panel_v=panel_v, panel_rank=panel_rank, trail_x=trail_x, trail_y=trail_y, trail_rank=trail_rank, tile_cols=tile_cols, owner=owner)


def clear_rows(factor, rank_value):
    kept_mask = jnp.arange(factor.shape[0], dtype=jnp.int32)[:, None] < rank_value
    return jnp.where(kept_mask, factor, jnp.zeros_like(factor))


def reference(panel_u, panel_v, panel_rank, trail_x, trail_y, trail_rank, tile_cols, owner):
    highest = lax.Precision.HIGHEST
    row_list = (jnp.arange(NT, dtype=jnp.int32) // TT).astype(jnp.int32)

    def tile_terms(inputs):
        left_rows, right_rows, trail_keep, row_tile, col_tile = inputs
        left_i = clear_rows(panel_u[row_tile], panel_rank[row_tile])
        right_i = clear_rows(panel_v[row_tile], panel_rank[row_tile])
        left_j = clear_rows(panel_u[col_tile], panel_rank[col_tile])
        right_j = clear_rows(panel_v[col_tile], panel_rank[col_tile])
        kept_x = clear_rows(left_rows, trail_keep)
        kept_y = clear_rows(right_rows, trail_keep)
        core = jnp.dot(right_i, right_j.T, preferred_element_type=jnp.float32)
        gram = jnp.dot(left_i, left_i.T, preferred_element_type=jnp.float32)
        part_left = jnp.dot(kept_x, left_i.T, preferred_element_type=jnp.float32)
        part_right = jnp.dot(kept_y, left_j.T, preferred_element_type=jnp.float32)
        own_left = jnp.dot(kept_x, kept_x.T, preferred_element_type=jnp.float32)
        own_right = jnp.dot(kept_y, kept_y.T, preferred_element_type=jnp.float32)
        left_cross = jnp.dot(part_left, core, precision=highest)
        left_new = jnp.dot(core.T, jnp.dot(gram, core, precision=highest), precision=highest)
        return own_left, left_cross, left_new, own_right, -part_right

    terms = lax.map(tile_terms, (trail_x, trail_y, trail_rank, row_list, tile_cols))
    owners = owner[:, 0].reshape(N_ROW, TT)
    order = jnp.arange(TT, dtype=jnp.int32)
    before = (owners[:, None, :] == owners[:, :, None]) & (order[None, None, :] < order[None, :, None])
    place_in = jnp.sum(before.astype(jnp.int32), axis=2)
    groups = jnp.arange(N_ROW, dtype=jnp.int32)[:, None]
    slots = ((groups * N_COL + owners) * CAP + place_in).reshape(-1).astype(jnp.int32)
    placed = [jnp.zeros((SLOTS, KMAX, KMAX), jnp.float32).at[slots].set(term) for term in terms]
    return (placed[0], placed[1], placed[2], placed[3], placed[4])
```

```python
import jax
import jax.numpy as jnp
from jax import lax
from jax.experimental import pallas as pl
from jax.experimental.pallas import tpu as pltpu
from jax.sharding import PartitionSpec as P

K = 128
S = 336
TILES = 8
PEERS = 64
COLS = 8
FULL = 10
HALF = K // 2
WIDE = (FULL + 1) * K
EARLY = 5 * K + 8
SPLIT = S - 16


def tile_dot(first, second):
    return lax.dot_general(
        first, second, (((0,), (0,)), ((), ())), preferred_element_type=jnp.float32
    )


def exact_dot(first, second, lhs_dim=1):
    return lax.dot_general(
        first,
        second,
        (((lhs_dim,), (0,)), ((), ())),
        precision=lax.Precision.HIGHEST,
        preferred_element_type=jnp.float32,
    )


def keep(block, rank):
    lane = lax.broadcasted_iota(jnp.int32, block.shape, block.ndim - 1)
    return jnp.where(lane < rank, block, jnp.zeros_like(block))


def owned_tiles(owner_ref, column):
    first = jnp.int32(-1)
    second = jnp.int32(-1)
    for t in range(TILES):
        mine = owner_ref[t] == column
        second = jnp.where(mine & (first >= 0), t, second)
        first = jnp.where(mine & (first < 0), t, first)
    return first, second


def early_kernel(owner_ref, rank_ref, panel_rank_ref, x_ref, y_ref, u_ref, out_ref, gram_ref):
    column = pl.program_id(0)
    left = keep(u_ref[...], panel_rank_ref[0])

    @pl.when(column == 0)
    def _():
        gram_ref[...] = tile_dot(left, left)

    row_at = lax.broadcasted_iota(jnp.int32, (K, K), 0)
    col_at = lax.broadcasted_iota(jnp.int32, (K, K), 1)
    out_ref[0, 4 * K : 5 * K, :] = gram_ref[...]
    out_ref[0, 5 * K : EARLY, :] = jnp.zeros((EARLY - 5 * K, K), jnp.float32)
    for place, t in enumerate(owned_tiles(owner_ref, column)):
        base = 2 * place * K

        @pl.when(t >= 0)
        def _():
            x = keep(x_ref[t], rank_ref[t])
            y = keep(y_ref[t], rank_ref[t])
            both = tile_dot(x, jnp.concatenate([x, left], axis=1))
            right = tile_dot(y, y)
            out_ref[0, base : base + K, :] = both[:, K:]
            out_ref[0, base + K : base + 2 * K, :] = jnp.where(
                row_at <= col_at, both[:, :K], right
            )
            out_ref[0, 5 * K + place : 5 * K + place + 1, :] = jnp.sum(
                jnp.where(row_at == col_at, right, 0.0), axis=0, keepdims=True
            )

        @pl.when(t < 0)
        def _():
            out_ref[0, base : base + 2 * K, :] = jnp.zeros((2 * K, K), jnp.float32)


def late_kernel(
    owner_ref, rank_ref, panel_rank_ref, got_ref, y_ref, v_ref, out_ref, whole, halves
):
    column = pl.program_id(0)

    @pl.when(column == 0)
    def _():
        for pair in range(PEERS // 2):
            rows = got_ref[16 * pair : 16 * pair + 16, :].astype(jnp.float32)
            for side in range(2):
                part = rows[8 * side : 8 * side + 8]
                peer = 2 * pair + side
                for q in range(FULL):
                    at = 8 * (peer * FULL + q)
                    whole[at : at + 8, :] = part[:, q * K : (q + 1) * K]
                halves[8 * peer : 8 * peer + 8, :] = part[:, FULL * K :]

    right = keep(v_ref[...], panel_rank_ref[0])
    low = lax.broadcasted_iota(jnp.int32, (16, K), 1) < HALF

    def panel_tile(t, which):
        body = whole[pl.ds(which * SPLIT * 8 + t, SPLIT, stride=8), :]
        start = which * PEERS * 4 + t
        end = jnp.where(
            low,
            halves[pl.ds(start, 16, stride=16), :],
            halves[pl.ds(start + 8, 16, stride=16), :],
        )
        return jnp.concatenate([body.astype(jnp.bfloat16), end.astype(jnp.bfloat16)], axis=0)

    for place, t in enumerate(owned_tiles(owner_ref, column)):
        base = 2 * place * K

        @pl.when(t >= 0)
        def _():
            y = keep(y_ref[t], rank_ref[t])
            out_ref[0, base : base + K, :] = tile_dot(right, panel_tile(t, 1))
            out_ref[0, base + K : base + 2 * K, :] = tile_dot(y, panel_tile(t, 0))

        @pl.when(t < 0)
        def _():
            out_ref[0, base : base + 2 * K, :] = jnp.zeros((2 * K, K), jnp.float32)


def final_kernel(early_ref, late_ref, lo_ref, lc_ref, ln_ref, ro_ref, rc_ref):
    row_at = lax.broadcasted_iota(jnp.int32, (K, K), 0)
    col_at = lax.broadcasted_iota(jnp.int32, (K, K), 1)
    gram = early_ref[4 * K : 5 * K, :]
    for place in range(2):
        base = 2 * place * K
        core = late_ref[0, base : base + K, :]
        part_right = late_ref[0, base + K : base + 2 * K, :]
        for c in range(1, COLS):
            core = core + late_ref[c, base : base + K, :]
            part_right = part_right + late_ref[c, base + K : base + 2 * K, :]
        part_left = early_ref[base : base + K, :]
        mixed = early_ref[base + K : base + 2 * K, :]
        turned = mixed.T
        diagonal = early_ref[5 * K + place : 5 * K + place + 1, :]
        lo_ref[place] = jnp.where(row_at <= col_at, mixed, turned)
        ro_ref[place] = jnp.where(
            row_at > col_at, mixed, jnp.where(row_at < col_at, turned, diagonal)
        )
        rc_ref[place] = -part_right
        lc_ref[place] = exact_dot(part_left, core)
        ln_ref[place] = exact_dot(core, exact_dot(gram, core), 0)


def smem():
    return pl.BlockSpec(memory_space=pltpu.SMEM)


def fixed(shape):
    return pl.BlockSpec(shape, lambda c: (0,) * len(shape))


def per_device(panel_u, panel_v, panel_rank, trail_x, trail_y, trail_rank, tile_cols, owner):
    xt = jnp.swapaxes(trail_x, 1, 2)
    yt = jnp.swapaxes(trail_y, 1, 2)
    ut = jnp.swapaxes(panel_u, 1, 2)[0]
    vt = jnp.swapaxes(panel_v, 1, 2)[0]
    owners = owner[:, 0]

    with jax.named_scope("slices_out"):
        kept = keep(jnp.stack([ut, vt]), panel_rank[0])
        whole = kept[:, :SPLIT].reshape(PEERS, FULL * K)
        ends = kept[:, SPLIT:].reshape(PEERS // 2, K)
        wanted = jnp.pad(tile_cols.astype(jnp.bfloat16), (0, HALF - TILES))
        wanted = jnp.broadcast_to(wanted, (PEERS // 2, HALF))
        tail = jnp.stack(
            [
                jnp.concatenate([ends[:, :HALF], wanted], axis=1),
                jnp.concatenate([wanted, ends[:, HALF:]], axis=1),
            ],
            axis=1,
        ).reshape(PEERS, K)
        slices = jnp.concatenate([whole, tail], axis=1)
        held = lax.all_to_all(slices.reshape(PEERS, 1, WIDE), "row", 0, 0).reshape(PEERS, WIDE)

    with jax.named_scope("first_products"):
        early, _ = pl.pallas_call(
            early_kernel,
            grid=(COLS,),
            in_specs=[
                smem(),
                smem(),
                smem(),
                fixed((TILES, S, K)),
                fixed((TILES, S, K)),
                fixed((S, K)),
            ],
            out_specs=[
                pl.BlockSpec((1, EARLY, K), lambda c: (c, 0, 0)),
                fixed((K, K)),
            ],
            out_shape=[
                jax.ShapeDtypeStruct((COLS, EARLY, K), jnp.float32),
                jax.ShapeDtypeStruct((K, K), jnp.float32),
            ],
            compiler_params=pltpu.CompilerParams(vmem_limit_bytes=32 * 1024 * 1024),
            name="first_products",
        )(owners, trail_rank, panel_rank, xt, yt, ut)
        early = lax.psum_scatter(early, "col", scatter_dimension=0, tiled=False)

    with jax.named_scope("tiles_asked_for"):
        at = jnp.where(lax.axis_index("row") % 2 == 0, FULL * K + HALF, FULL * K)
        asked = lax.dynamic_slice(held, (0, at), (PEERS, TILES)).astype(jnp.int32)
        chosen = asked.reshape(PEERS * TILES, 1) == lax.broadcasted_iota(
            jnp.int32, (PEERS * TILES, PEERS), 1
        )
        sent = jnp.dot(
            chosen.astype(jnp.bfloat16), held, preferred_element_type=jnp.float32
        ).astype(jnp.bfloat16)
        got = lax.all_to_all(sent.reshape(PEERS, TILES, WIDE), "row", 0, 0)

    with jax.named_scope("second_products"):
        late = pl.pallas_call(
            late_kernel,
            grid=(COLS,),
            in_specs=[
                smem(),
                smem(),
                smem(),
                fixed((PEERS * TILES, WIDE)),
                fixed((TILES, S, K)),
                fixed((S, K)),
            ],
            out_specs=pl.BlockSpec((1, 4 * K, K), lambda c: (c, 0, 0)),
            out_shape=jax.ShapeDtypeStruct((COLS, 4 * K, K), jnp.float32),
            scratch_shapes=[
                pltpu.VMEM((PEERS * FULL * TILES, K), jnp.float32),
                pltpu.VMEM((PEERS * TILES, K), jnp.float32),
            ],
            compiler_params=pltpu.CompilerParams(vmem_limit_bytes=32 * 1024 * 1024),
            name="second_products",
        )(owners, trail_rank, panel_rank, got.reshape(PEERS * TILES, WIDE), yt, vt)
        late = lax.all_to_all(late, "col", 0, 0)

    with jax.named_scope("owned_results"):
        result = jax.ShapeDtypeStruct((2, K, K), jnp.float32)
        return pl.pallas_call(
            final_kernel,
            out_shape=(result,) * 5,
            compiler_params=pltpu.CompilerParams(vmem_limit_bytes=32 * 1024 * 1024),
            name="owned_results",
        )(early, late)


def solution(mesh):
    placed = (
        P("row", None, "col"),
        P("row", None, "col"),
        P("row"),
        P("row", None, "col"),
        P("row", None, "col"),
        P("row"),
        P("row"),
        P("row", None),
    )
    return jax.shard_map(
        per_device,
        mesh=mesh,
        in_specs=placed,
        out_specs=(P(("row", "col"), None, None),) * 5,
        check_vma=False,
    )
```

```python
import jax
import jax.numpy as jnp
from jax import lax
from jax.experimental import pallas as pl
from jax.experimental.pallas import tpu as pltpu
from jax.sharding import PartitionSpec as P

K = 128
S = 336
TILES = 8
PEERS = 64
COLS = 8
EACH = 10
SLICED = EACH * PEERS // 2
SHARED = S - SLICED
WIDE = (EACH + 1) * K
BLOCK = 16
HALF = K // 2
LONG = 3 * K
PART = K // COLS
EARLY = TILES * PART
FIRST = EARLY + 8
SECOND = EARLY + PART
OWNED = 8 * PART + PART + 8
EARLY_AT = [
    slice(at, at + 2 * PART)
    for base in (0, FIRST)
    for at in range(base, base + EARLY, 2 * PART)
]
VMEM = 32 * 1024 * 1024


def tile_dot(first, second):
    return lax.dot_general(
        first, second, (((0,), (0,)), ((), ())), preferred_element_type=jnp.float32
    )


def plain_dot(first, second):
    return jnp.dot(first, second, preferred_element_type=jnp.float32)


def exact_dot(first, second, lhs_dim=1):
    return lax.dot_general(
        first,
        second,
        (((lhs_dim,), (0,)), ((), ())),
        precision=lax.Precision.HIGHEST,
        preferred_element_type=jnp.float32,
    )


def keep(block, rank):
    lane = lax.broadcasted_iota(jnp.int32, block.shape, block.ndim - 1)
    return jnp.where(lane < rank, block, jnp.zeros_like(block))


def owned_tiles(owner_ref, column):
    first = jnp.int32(-1)
    second = jnp.int32(-1)
    for t in range(TILES):
        mine = owner_ref[t] == column
        second = jnp.where(mine & (first >= 0), t, second)
        first = jnp.where(mine & (first < 0), t, first)
    return first, second


def slices_kernel(cols_ref, kept_ref, slices_ref, rows, blocks):
    lane = lax.broadcasted_iota(jnp.int32, (SHARED, K), 1)
    wanted = jnp.zeros((SHARED, K), jnp.int32)
    for t in range(TILES):
        wanted = jnp.where(lane % HALF == t, cols_ref[t], wanted)
    wanted = wanted.astype(jnp.float32)
    blocks[...] = jnp.zeros_like(blocks)
    for which in range(2):
        kept = kept_ref[which]
        rows[which * SLICED : (which + 1) * SLICED, :] = kept[:SLICED].astype(jnp.float32)
        ends = kept[SLICED:].astype(jnp.float32)
        at = which * PEERS // 2 * BLOCK + EACH
        blocks[pl.ds(at, SHARED, stride=2 * BLOCK), :] = jnp.where(lane < HALF, ends, wanted)
        blocks[pl.ds(at + BLOCK, SHARED, stride=2 * BLOCK), :] = jnp.where(
            lane < HALF, wanted, ends
        )
    for q in range(EACH):
        blocks[pl.ds(q, PEERS, stride=BLOCK), :] = rows[pl.ds(q, PEERS, stride=EACH), :]
    slices_ref[...] = blocks[...].astype(jnp.bfloat16)


def turned(block):
    filler = jnp.zeros((LONG - S, K), block.dtype)
    return jnp.concatenate([block, filler], axis=0).T


def early_kernel(
    rank_ref,
    kept_ref,
    x_ref,
    y_ref,
    first_sent,
    first_kept,
    second_sent,
    second_kept,
    right_turned,
    y_turned,
    products,
    diagonals,
    gram,
):
    left = kept_ref[0]
    right_turned[...] = turned(kept_ref[1])
    gram[...] = tile_dot(left, left)
    row_at = lax.broadcasted_iota(jnp.int32, (K, K), 0)
    col_at = lax.broadcasted_iota(jnp.int32, (K, K), 1)
    for t in range(TILES):
        x = keep(x_ref[t], rank_ref[t])
        y = keep(y_ref[t], rank_ref[t])
        y_turned[t] = turned(y)
        both = tile_dot(x, jnp.concatenate([x, left], axis=1))
        right = tile_dot(y, y)
        products[t, 0] = both[:, K:]
        products[t, 1] = jnp.where(row_at <= col_at, both[:, :K], right)
        diagonal = jnp.sum(jnp.where(row_at == col_at, right, 0.0), axis=0, keepdims=True)
        diagonals[t] = jnp.broadcast_to(diagonal, (8, K))

    here = lax.axis_index("col")
    firsts = [(first_kept, 0), (first_sent, 0), (first_sent, 1), (first_kept, 1)]
    seconds = [(second_kept, 0), (second_kept, 1), (second_sent, 1), (second_sent, 0)]
    for away in range(COLS):
        column = here ^ away
        start = pl.multiple_of(column * PART, PART)
        along, across = away // 2, away % 2
        for low, (ref, at) in ((0, firsts[along]), (TILES // 2, seconds[along])):
            for n in range(TILES):
                ref[at, across, n * PART : (n + 1) * PART, :] = products[
                    low + n // 2, n % 2, pl.ds(start, PART), :
                ]
        ref, at = firsts[along]
        ref[at, across, EARLY:, :] = diagonals[column]
        ref, at = seconds[along]
        ref[at, across, EARLY:, :] = gram[pl.ds(start, PART), :]


def late_kernel(
    got_ref, right_ref, y_ref, out_ref, rows, halves
):
    for pair in range(PEERS // 2):
        part = got_ref[16 * pair : 16 * pair + 16, :].astype(jnp.float32)
        for side in range(2):
            peer = 2 * pair + side
            mine = part[8 * side : 8 * side + 8]
            for q in range(EACH):
                at = 8 * (peer * EACH + q)
                rows[at : at + 8, :] = mine[:, q * K : (q + 1) * K]
            halves[8 * peer : 8 * peer + 8, :] = mine[:, EACH * K :]
    right = right_ref[...]
    filler = jnp.zeros((LONG - S, K), jnp.bfloat16)
    low = lax.broadcasted_iota(jnp.int32, (SHARED, K), 1) < HALF

    def panel_tile(t, which):
        body = rows[pl.ds(which * SLICED * 8 + t, SLICED, stride=8), :]
        at = which * PEERS * 4 + t
        end = jnp.where(
            low,
            halves[pl.ds(at, SHARED, stride=16), :],
            halves[pl.ds(at + 8, SHARED, stride=16), :],
        )
        return jnp.concatenate(
            [body.astype(jnp.bfloat16), end.astype(jnp.bfloat16), filler], axis=0
        )

    for t in range(TILES):
        core = plain_dot(right, panel_tile(t, 1))
        part_right = plain_dot(y_ref[t], panel_tile(t, 0))
        for c in range(COLS):
            base = 2 * t * PART
            out_ref[c, base : base + PART, :] = core[c * PART : (c + 1) * PART]
            out_ref[c, base + PART : base + 2 * PART, :] = part_right[c * PART : (c + 1) * PART]


def route_kernel(owner_ref, kept_ref, came_ref, late_ref, out_ref, sums):
    for t in range(TILES):
        base = 2 * t * PART
        sums[t, : 2 * PART, :] = kept_ref[EARLY_AT[t], :] + came_ref[EARLY_AT[t], :]
        total = late_ref[0, base : base + 2 * PART, :]
        for c in range(1, COLS):
            total = total + late_ref[c, base : base + 2 * PART, :]
        sums[t, 2 * PART :, :] = total
    diagonal = kept_ref[EARLY:FIRST, :] + came_ref[EARLY:FIRST, :]
    gram = kept_ref[FIRST + EARLY :, :] + came_ref[FIRST + EARLY :, :]
    for column in range(COLS):
        for place, t in enumerate(owned_tiles(owner_ref, column)):
            there = slice(4 * place * PART, 4 * (place + 1) * PART)

            @pl.when(t >= 0)
            def _():
                out_ref[column, there, :] = sums[t]

            @pl.when(t < 0)
            def _():
                out_ref[column, there, :] = jnp.zeros((4 * PART, K), jnp.float32)

        out_ref[column, 8 * PART : 9 * PART, :] = gram
        out_ref[column, 9 * PART :, :] = diagonal


def final_kernel(owner_ref, got_ref, lo_ref, lc_ref, ln_ref, ro_ref, rc_ref):
    row_at = lax.broadcasted_iota(jnp.int32, (K, K), 0)
    col_at = lax.broadcasted_iota(jnp.int32, (K, K), 1)

    def whole(at):
        return jnp.concatenate(
            [got_ref[c, at * PART : (at + 1) * PART, :] for c in range(COLS)], axis=0
        )

    gram = whole(8)
    for place, t in enumerate(owned_tiles(owner_ref, lax.axis_index("col"))):
        part_left = whole(4 * place)
        mixed = whole(4 * place + 1)
        core = whole(4 * place + 2)
        part_right = whole(4 * place + 3)
        diagonal = jnp.where(t >= 0, got_ref[jnp.maximum(t, 0), 9 * PART :, :][:1], 0.0)
        across = mixed.T
        lo_ref[place] = jnp.where(row_at <= col_at, mixed, across)
        ro_ref[place] = jnp.where(
            row_at > col_at, mixed, jnp.where(row_at < col_at, across, diagonal)
        )
        rc_ref[place] = -part_right
        lc_ref[place] = exact_dot(part_left, core)
        ln_ref[place] = exact_dot(core, exact_dot(gram, core), 0)


def swapped(block, away):
    return lax.ppermute(block, "col", [(c, c ^ away) for c in range(COLS)])


def cost(micros):
    return pl.CostEstimate(flops=micros * 1000000000, bytes_accessed=0, transcendentals=0)


def smem(count):
    return [pl.BlockSpec(memory_space=pltpu.SMEM)] * count


def vmem(count):
    return [pl.BlockSpec(memory_space=pltpu.VMEM)] * count


def per_device(panel_u, panel_v, panel_rank, trail_x, trail_y, trail_rank, tile_cols, owner):
    params = pltpu.CompilerParams(vmem_limit_bytes=VMEM)
    xt = jnp.swapaxes(trail_x, 1, 2)
    yt = jnp.swapaxes(trail_y, 1, 2)
    ut = jnp.swapaxes(panel_u, 1, 2)[0]
    vt = jnp.swapaxes(panel_v, 1, 2)[0]
    owners = owner[:, 0]

    with jax.named_scope("slices_out"):
        kept = keep(jnp.stack([ut, vt]), panel_rank[0])
        slices = pl.pallas_call(
            slices_kernel,
            in_specs=smem(1) + vmem(1),
            out_shape=jax.ShapeDtypeStruct((PEERS * BLOCK, K), jnp.bfloat16),
            scratch_shapes=[
                pltpu.VMEM((2 * SLICED, K), jnp.float32),
                pltpu.VMEM((PEERS * BLOCK, K), jnp.float32),
            ],
            compiler_params=params,
            cost_estimate=cost(1),
            name="slices_out",
        )(tile_cols, kept)
        held = lax.all_to_all(slices.reshape(PEERS, BLOCK, K), "row", 0, 0)
        held = held.reshape(PEERS, BLOCK * K)

    with jax.named_scope("first_products"):
        first = jax.ShapeDtypeStruct((2, 2, FIRST, K), jnp.float32)
        second = jax.ShapeDtypeStruct((2, 2, SECOND, K), jnp.float32)
        *pieces, right_turned, y_turned = pl.pallas_call(
            early_kernel,
            in_specs=smem(1) + vmem(3),
            out_shape=[
                first,
                first,
                second,
                second,
                jax.ShapeDtypeStruct((K, LONG), jnp.bfloat16),
                jax.ShapeDtypeStruct((TILES, K, LONG), jnp.bfloat16),
            ],
            scratch_shapes=[
                pltpu.VMEM((TILES, 2, K, K), jnp.float32),
                pltpu.VMEM((TILES, 8, K), jnp.float32),
                pltpu.VMEM((K, K), jnp.float32),
            ],
            compiler_params=params,
            cost_estimate=cost(4),
            name="first_products",
        )(trail_rank, kept, xt, yt)
        held, *_ = lax.optimization_barrier((held, *pieces))

    with jax.named_scope("first_sum"):
        first_sent, first_kept, second_sent, second_kept = pieces
        first = first_kept + swapped(first_sent, 2)
        second = second_kept + swapped(second_sent, 6)
        first = first[0] + swapped(first[1], 6)
        second = second[0] + swapped(second[1], 2)
        early_kept = jnp.concatenate([first[0], second[0]])
        early_came = swapped(jnp.concatenate([first[1], second[1]]), 1)

    with jax.named_scope("tiles_asked_for"):
        at = jnp.where(lax.axis_index("row") % 2 == 0, EACH * K + HALF, EACH * K)
        asked = lax.dynamic_slice(held, (0, at), (PEERS, TILES)).astype(jnp.int32)
        chosen = asked.reshape(PEERS * TILES, 1) == lax.broadcasted_iota(
            jnp.int32, (PEERS * TILES, PEERS), 1
        )
        sent = jnp.dot(
            chosen.astype(jnp.bfloat16), held[:, :WIDE], preferred_element_type=jnp.float32
        ).astype(jnp.bfloat16)
        got = lax.all_to_all(sent.reshape(PEERS, TILES, WIDE), "row", 0, 0)
        got, early_came = lax.optimization_barrier((got, early_came))

    with jax.named_scope("second_products"):
        late = pl.pallas_call(
            late_kernel,
            in_specs=vmem(3),
            out_shape=jax.ShapeDtypeStruct((COLS, 2 * K, K), jnp.float32),
            scratch_shapes=[
                pltpu.VMEM((PEERS * EACH * TILES, K), jnp.float32),
                pltpu.VMEM((PEERS * TILES, K), jnp.float32),
            ],
            compiler_params=params,
            cost_estimate=cost(4),
            name="second_products",
        )(got.reshape(PEERS * TILES, WIDE), right_turned, y_turned)
        late = lax.all_to_all(late, "col", 0, 0)

    with jax.named_scope("parts_to_owners"):
        owned = pl.pallas_call(
            route_kernel,
            in_specs=smem(1) + vmem(3),
            out_shape=jax.ShapeDtypeStruct((COLS, OWNED, K), jnp.float32),
            scratch_shapes=[pltpu.VMEM((TILES, 4 * PART, K), jnp.float32)],
            compiler_params=params,
            cost_estimate=cost(1),
            name="parts_to_owners",
        )(owners, early_kept, early_came, late)
        owned = lax.all_to_all(owned, "col", 0, 0)

    with jax.named_scope("owned_results"):
        result = jax.ShapeDtypeStruct((2, K, K), jnp.float32)
        return pl.pallas_call(
            final_kernel,
            in_specs=smem(1) + vmem(1),
            out_shape=(result,) * 5,
            compiler_params=params,
            name="owned_results",
        )(owners, owned)


def solution(mesh):
    placed = (
        P("row", None, "col"),
        P("row", None, "col"),
        P("row"),
        P("row", None, "col"),
        P("row", None, "col"),
        P("row"),
        P("row"),
        P("row", None),
    )
    return jax.shard_map(
        per_device,
        mesh=mesh,
        in_specs=placed,
        out_specs=(P(("row", "col"), None, None),) * 5,
        check_vma=False,
    )
```

```python
import jax
import jax.numpy as jnp
from jax import lax
from jax.experimental import pallas as pl
from jax.experimental.pallas import tpu as pltpu
from jax.sharding import PartitionSpec as P

K = 128
S = 336
TILES = 8
PEERS = 64
COLS = 8
HOLDERS = PEERS // 2
EACH = 10
SLICED = EACH * HOLDERS
SHARED = S - SLICED
LAST = 2 * EACH
WIDE = (LAST + 1) * K
BLOCK = 24
LONG = 3 * K
PART = K // COLS
EARLY = TILES * PART
FIRST = EARLY + 8
SECOND = EARLY + PART
OWNED = 8 * PART + PART + 8
EARLY_AT = [
    slice(at, at + 2 * PART)
    for base in (0, FIRST)
    for at in range(base, base + EARLY, 2 * PART)
]
VMEM = 32 * 1024 * 1024


def tile_dot(first, second):
    return lax.dot_general(
        first, second, (((0,), (0,)), ((), ())), preferred_element_type=jnp.float32
    )


def plain_dot(first, second):
    return jnp.dot(first, second, preferred_element_type=jnp.float32)


def exact_dot(first, second, lhs_dim=1):
    return lax.dot_general(
        first,
        second,
        (((lhs_dim,), (0,)), ((), ())),
        precision=lax.Precision.HIGHEST,
        preferred_element_type=jnp.float32,
    )


def keep(block, rank):
    lane = lax.broadcasted_iota(jnp.int32, block.shape, block.ndim - 1)
    return jnp.where(lane < rank, block, jnp.zeros_like(block))


def owned_tiles(owner_ref, column):
    first = jnp.int32(-1)
    second = jnp.int32(-1)
    for t in range(TILES):
        mine = owner_ref[t] == column
        second = jnp.where(mine & (first >= 0), t, second)
        first = jnp.where(mine & (first < 0), t, first)
    return first, second


def slices_kernel(kept_ref, slices_ref, rows, ends, blocks):
    wanted = kept_ref[2 * S : 2 * S + 16, :].astype(jnp.float32)
    wanted = jnp.concatenate([wanted, wanted], axis=0)
    for which in range(2):
        kept = kept_ref[which * S : (which + 1) * S, :]
        rows[which * SLICED : (which + 1) * SLICED, :] = kept[:SLICED].astype(jnp.float32)
        ends[which * SHARED : (which + 1) * SHARED, :] = kept[SLICED:].astype(jnp.float32)
    for core in range(2):

        def place(at, part):
            blocks[pl.ds(core * BLOCK + at, HOLDERS, stride=2 * BLOCK), :] = part

        for which in range(2):
            for q in range(EACH):
                place(which * EACH + q, rows[pl.ds(which * SLICED + q, HOLDERS, stride=EACH), :])
        place(LAST, ends[...])
        place(LAST + 1, wanted)
        for at in range(LAST + 2, BLOCK):
            place(at, jnp.zeros((HOLDERS, K), jnp.float32))
    slices_ref[...] = blocks[...].astype(jnp.bfloat16)


def turned(block):
    filler = jnp.zeros((LONG - S, K), block.dtype)
    return jnp.concatenate([block, filler], axis=0).T


def early_kernel(
    owner_ref,
    rank_ref,
    kept_ref,
    x_ref,
    y_ref,
    first_sent,
    first_kept,
    second_sent,
    second_kept,
    right_turned,
    y_turned,
    products,
    diagonals,
    gram,
):
    left = kept_ref[:S]
    right_turned[...] = turned(kept_ref[S : 2 * S])
    gram[...] = tile_dot(left, left)
    row_at = lax.broadcasted_iota(jnp.int32, (K, K), 0)
    col_at = lax.broadcasted_iota(jnp.int32, (K, K), 1)
    for t in range(TILES):
        x = keep(x_ref[t], rank_ref[t])
        y = keep(y_ref[t], rank_ref[t])
        y_turned[t] = turned(y)
        both = tile_dot(x, jnp.concatenate([x, left], axis=1))
        right = tile_dot(y, y)
        products[t, 0] = both[:, K:]
        products[t, 1] = jnp.where(row_at <= col_at, both[:, :K], right)
        diagonal = jnp.sum(jnp.where(row_at == col_at, right, 0.0), axis=0, keepdims=True)
        diagonals[t] = jnp.broadcast_to(diagonal, (8, K))

    here = lax.axis_index("col")
    firsts = [(first_kept, 0), (first_sent, 0), (first_sent, 1), (first_kept, 1)]
    seconds = [(second_kept, 0), (second_kept, 1), (second_sent, 1), (second_sent, 0)]
    for away in range(COLS):
        column = here ^ away
        start = pl.multiple_of(column * PART, PART)
        along, across = away // 2, away % 2
        for low, (ref, at) in ((0, firsts[along]), (TILES // 2, seconds[along])):
            for n in range(TILES):
                ref[at, across, n * PART : (n + 1) * PART, :] = products[
                    low + n // 2, n % 2, pl.ds(start, PART), :
                ]
        ref, at = firsts[along]
        ref[at, across, EARLY:, :] = diagonals[column]
        ref, at = seconds[along]
        ref[at, across, EARLY:, :] = gram[pl.ds(start, PART), :]


def late_kernel(
    got_ref, right_ref, y_ref, out_ref, rows, ends
):
    for pair in range(HOLDERS // 2):
        part = got_ref[16 * pair : 16 * pair + 16, :].astype(jnp.float32)
        for side in range(2):
            holder = 2 * pair + side
            mine = part[8 * side : 8 * side + 8]
            for which in range(2):
                for q in range(EACH):
                    at = 8 * (which * SLICED + holder * EACH + q)
                    from_lane = (which * EACH + q) * K
                    rows[at : at + 8, :] = mine[:, from_lane : from_lane + K]
            ends[8 * holder : 8 * holder + 8, :] = mine[:, LAST * K :]
    right = right_ref[...]
    filler = jnp.zeros((LONG - S, K), jnp.bfloat16)

    def panel_tile(t, which):
        body = rows[pl.ds(8 * which * SLICED + t, SLICED, stride=8), :]
        end = ends[pl.ds(8 * which * SHARED + t, SHARED, stride=8), :]
        return jnp.concatenate(
            [body.astype(jnp.bfloat16), end.astype(jnp.bfloat16), filler], axis=0
        )

    for t in range(TILES):
        core = plain_dot(right, panel_tile(t, 1))
        part_right = plain_dot(y_ref[t], panel_tile(t, 0))
        for c in range(COLS):
            base = 2 * t * PART
            out_ref[c, base : base + PART, :] = core[c * PART : (c + 1) * PART]
            out_ref[c, base + PART : base + 2 * PART, :] = part_right[c * PART : (c + 1) * PART]


def route_kernel(owner_ref, kept_ref, came_ref, late_ref, out_ref, sums):
    for t in range(TILES):
        base = 2 * t * PART
        sums[t, : 2 * PART, :] = kept_ref[EARLY_AT[t], :] + came_ref[EARLY_AT[t], :]
        total = late_ref[0, base : base + 2 * PART, :]
        for c in range(1, COLS):
            total = total + late_ref[c, base : base + 2 * PART, :]
        sums[t, 2 * PART :, :] = total
    diagonal = kept_ref[EARLY:FIRST, :] + came_ref[EARLY:FIRST, :]
    gram = kept_ref[FIRST + EARLY :, :] + came_ref[FIRST + EARLY :, :]
    for column in range(COLS):
        for place, t in enumerate(owned_tiles(owner_ref, column)):
            there = slice(4 * place * PART, 4 * (place + 1) * PART)

            @pl.when(t >= 0)
            def _():
                out_ref[column, there, :] = sums[t]

            @pl.when(t < 0)
            def _():
                out_ref[column, there, :] = jnp.zeros((4 * PART, K), jnp.float32)

        out_ref[column, 8 * PART : 9 * PART, :] = gram
        out_ref[column, 9 * PART :, :] = jnp.zeros((8, K), jnp.float32)

    here = lax.axis_index("col")
    place = jnp.int32(0)
    for t in range(TILES):
        place = place + ((t < here) & (owner_ref[t] == owner_ref[here])).astype(jnp.int32)
    row_at = lax.broadcasted_iota(jnp.int32, (8, K), 0)
    out_ref[owner_ref[here], 9 * PART :, :] = jnp.where(row_at == place, diagonal, 0.0)


def final_kernel(got_ref, lo_ref, lc_ref, ln_ref, ro_ref, rc_ref):
    row_at = lax.broadcasted_iota(jnp.int32, (K, K), 0)
    col_at = lax.broadcasted_iota(jnp.int32, (K, K), 1)

    def whole(at):
        return jnp.concatenate(
            [got_ref[c, at * PART : (at + 1) * PART, :] for c in range(COLS)], axis=0
        )

    gram = whole(8)
    diagonals = got_ref[0, 9 * PART :, :]
    for c in range(1, COLS):
        diagonals = diagonals + got_ref[c, 9 * PART :, :]
    for place in range(2):
        part_left = whole(4 * place)
        mixed = whole(4 * place + 1)
        core = whole(4 * place + 2)
        part_right = whole(4 * place + 3)
        diagonal = diagonals[place : place + 1]
        across = mixed.T
        lo_ref[place] = jnp.where(row_at <= col_at, mixed, across)
        ro_ref[place] = jnp.where(
            row_at > col_at, mixed, jnp.where(row_at < col_at, across, diagonal)
        )
        rc_ref[place] = -part_right
        lc_ref[place] = exact_dot(part_left, core)
        ln_ref[place] = exact_dot(core, exact_dot(gram, core), 0)


def swapped(block, away):
    return lax.ppermute(block, "col", [(c, c ^ away) for c in range(COLS)])


def cost(micros):
    return pl.CostEstimate(flops=micros * 1000000000, bytes_accessed=0, transcendentals=0)


def smem(count):
    return [pl.BlockSpec(memory_space=pltpu.SMEM)] * count


def vmem(count):
    return [pl.BlockSpec(memory_space=pltpu.VMEM)] * count


def per_device(panel_u, panel_v, panel_rank, trail_x, trail_y, trail_rank, tile_cols, owner):
    params = pltpu.CompilerParams(vmem_limit_bytes=VMEM)
    xt = jnp.swapaxes(trail_x, 1, 2)
    yt = jnp.swapaxes(trail_y, 1, 2)
    ut = jnp.swapaxes(panel_u, 1, 2)[0]
    vt = jnp.swapaxes(panel_v, 1, 2)[0]
    owners = owner[:, 0]

    with jax.named_scope("slices_out"):
        wanted = jnp.pad(tile_cols.astype(jnp.bfloat16), (0, K - TILES))
        kept = jnp.concatenate(
            [
                keep(ut, panel_rank[0]),
                keep(vt, panel_rank[0]),
                jnp.broadcast_to(wanted, (16, K)),
            ]
        )
        slices = pl.pallas_call(
            slices_kernel,
            in_specs=vmem(1),
            out_shape=jax.ShapeDtypeStruct((PEERS * BLOCK, K), jnp.bfloat16),
            scratch_shapes=[
                pltpu.VMEM((2 * SLICED, K), jnp.float32),
                pltpu.VMEM((2 * SHARED, K), jnp.float32),
                pltpu.VMEM((PEERS * BLOCK, K), jnp.float32),
            ],
            compiler_params=params,
            cost_estimate=cost(1),
            name="slices_out",
        )(kept)
        held = lax.all_to_all(slices.reshape(PEERS, BLOCK, K), "row", 0, 0)
        held = held.reshape(PEERS, BLOCK * K)

    with jax.named_scope("first_products"):
        first = jax.ShapeDtypeStruct((2, 2, FIRST, K), jnp.float32)
        second = jax.ShapeDtypeStruct((2, 2, SECOND, K), jnp.float32)
        *pieces, right_turned, y_turned = pl.pallas_call(
            early_kernel,
            in_specs=smem(2) + vmem(3),
            out_shape=[
                first,
                first,
                second,
                second,
                jax.ShapeDtypeStruct((K, LONG), jnp.bfloat16),
                jax.ShapeDtypeStruct((TILES, K, LONG), jnp.bfloat16),
            ],
            scratch_shapes=[
                pltpu.VMEM((TILES, 2, K, K), jnp.float32),
                pltpu.VMEM((TILES, 8, K), jnp.float32),
                pltpu.VMEM((K, K), jnp.float32),
            ],
            compiler_params=params,
            cost_estimate=cost(4),
            name="first_products",
        )(owners, trail_rank, kept, xt, yt)

    held, *_ = lax.optimization_barrier((held, *pieces))

    with jax.named_scope("first_sum"):
        first_sent, first_kept, second_sent, second_kept = pieces
        first = first_kept + swapped(first_sent, 2)
        second = second_kept + swapped(second_sent, 6)
        first = first[0] + swapped(first[1], 6)
        second = second[0] + swapped(second[1], 2)
        early_kept = jnp.concatenate([first[0], second[0]])
        early_came = swapped(jnp.concatenate([first[1], second[1]]), 1)

    with jax.named_scope("tiles_asked_for"):
        asked = held[:, WIDE : WIDE + TILES].reshape(HOLDERS, 2, TILES)
        asked = jnp.where(lax.axis_index("row") % 2 == 0, asked[:, 0], asked[:, 1])
        chosen = asked.astype(jnp.int32).reshape(HOLDERS * TILES, 1) == lax.broadcasted_iota(
            jnp.int32, (HOLDERS * TILES, PEERS), 1
        )
        sent = jnp.dot(
            chosen.astype(jnp.bfloat16), held[:, :WIDE], preferred_element_type=jnp.float32
        ).astype(jnp.bfloat16)
        same_core = [list(range(core, PEERS, 2)) for core in range(2)]
        got = lax.all_to_all(
            sent.reshape(HOLDERS, TILES, WIDE), "row", 0, 0, axis_index_groups=same_core
        )
        got, early_kept, early_came, owners = lax.optimization_barrier(
            (got, early_kept, early_came, owners)
        )

    with jax.named_scope("second_products"):
        late = pl.pallas_call(
            late_kernel,
            in_specs=vmem(3),
            out_shape=jax.ShapeDtypeStruct((COLS, 2 * K, K), jnp.float32),
            scratch_shapes=[
                pltpu.VMEM((2 * SLICED * TILES, K), jnp.float32),
                pltpu.VMEM((HOLDERS * TILES, K), jnp.float32),
            ],
            compiler_params=params,
            cost_estimate=cost(4),
            name="second_products",
        )(got.reshape(HOLDERS * TILES, WIDE), right_turned, y_turned)
        late = lax.all_to_all(late, "col", 0, 0)

    with jax.named_scope("parts_to_owners"):
        owned = pl.pallas_call(
            route_kernel,
            in_specs=smem(1) + vmem(3),
            out_shape=jax.ShapeDtypeStruct((COLS, OWNED, K), jnp.float32),
            scratch_shapes=[pltpu.VMEM((TILES, 4 * PART, K), jnp.float32)],
            compiler_params=params,
            cost_estimate=cost(1),
            name="parts_to_owners",
        )(owners, early_kept, early_came, late)
        owned = lax.all_to_all(owned, "col", 0, 0)

    with jax.named_scope("owned_results"):
        result = jax.ShapeDtypeStruct((2, K, K), jnp.float32)
        return pl.pallas_call(
            final_kernel,
            out_shape=(result,) * 5,
            compiler_params=params,
            name="owned_results",
        )(owned)


def solution(mesh):
    placed = (
        P("row", None, "col"),
        P("row", None, "col"),
        P("row"),
        P("row", None, "col"),
        P("row", None, "col"),
        P("row"),
        P("row"),
        P("row", None),
    )
    return jax.shard_map(
        per_device,
        mesh=mesh,
        in_specs=placed,
        out_specs=(P(("row", "col"), None, None),) * 5,
        check_vma=False,
    )
```

```python
import jax
import jax.numpy as jnp
from jax import lax
from jax.experimental import pallas as pl
from jax.experimental.pallas import tpu as pltpu
from jax.sharding import PartitionSpec as P

K = 128
S = 336
TILES = 8
PEERS = 64
COLS = 8
HOLDERS = PEERS // 2
EACH = 10
SLICED = EACH * HOLDERS
SHARED = S - SLICED
LAST = 2 * EACH
WIDE = (LAST + 1) * K
BLOCK = 24
LONG = 3 * K
PART = K // COLS
EARLY = TILES * PART
FIRST = EARLY + 8
SECOND = EARLY + PART
OWNED = 8 * PART + PART + 8
EARLY_AT = [
    slice(at, at + 2 * PART)
    for base in (0, FIRST)
    for at in range(base, base + EARLY, 2 * PART)
]
SPARE = 16
VMEM = 32 * 1024 * 1024


def tile_dot(first, second):
    return lax.dot_general(
        first, second, (((0,), (0,)), ((), ())), preferred_element_type=jnp.float32
    )


def plain_dot(first, second):
    return jnp.dot(first, second, preferred_element_type=jnp.float32)


def exact_dot(first, second, lhs_dim=1):
    return lax.dot_general(
        first,
        second,
        (((lhs_dim,), (0,)), ((), ())),
        precision=lax.Precision.HIGHEST,
        preferred_element_type=jnp.float32,
    )


def keep(block, rank):
    lane = lax.broadcasted_iota(jnp.int32, block.shape, block.ndim - 1)
    return jnp.where(lane < rank, block, jnp.zeros_like(block))


def owned_tiles(owner_ref, column):
    first = jnp.int32(-1)
    second = jnp.int32(-1)
    for t in range(TILES):
        mine = owner_ref[t] == column
        second = jnp.where(mine & (first >= 0), t, second)
        first = jnp.where(mine & (first < 0), t, first)
    return first, second


def slices_kernel(kept_ref, slices_ref, rows, ends, blocks):
    wanted = kept_ref[2 * S : 2 * S + 16, :].astype(jnp.float32)
    wanted = jnp.concatenate([wanted, wanted], axis=0)
    for which in range(2):
        kept = kept_ref[which * S : (which + 1) * S, :]
        rows[which * SLICED : (which + 1) * SLICED, :] = kept[:SLICED].astype(jnp.float32)
        ends[which * SHARED : (which + 1) * SHARED, :] = kept[SLICED:].astype(jnp.float32)
    for core in range(2):

        def place(at, part):
            blocks[pl.ds(core * BLOCK + at, HOLDERS, stride=2 * BLOCK), :] = part

        for which in range(2):
            for q in range(EACH):
                place(which * EACH + q, rows[pl.ds(which * SLICED + q, HOLDERS, stride=EACH), :])
        place(LAST, ends[...])
        place(LAST + 1, wanted)
        for at in range(LAST + 2, BLOCK):
            place(at, jnp.zeros((HOLDERS, K), jnp.float32))
    slices_ref[...] = blocks[: PEERS * BLOCK, :].astype(jnp.bfloat16)


def turned(block):
    filler = jnp.zeros((LONG - S, K), block.dtype)
    return jnp.concatenate([block, filler], axis=0).T


def early_kernel(
    owner_ref,
    rank_ref,
    kept_ref,
    x_ref,
    y_ref,
    first_sent,
    first_kept,
    second_sent,
    second_kept,
    right_turned,
    y_turned,
    products,
    diagonals,
    gram,
):
    left = kept_ref[:S]
    right_turned[...] = turned(kept_ref[S : 2 * S])
    gram[...] = tile_dot(left, left)
    row_at = lax.broadcasted_iota(jnp.int32, (K, K), 0)
    col_at = lax.broadcasted_iota(jnp.int32, (K, K), 1)
    for t in range(TILES):
        x = keep(x_ref[t], rank_ref[t])
        y = keep(y_ref[t], rank_ref[t])
        y_turned[t] = turned(y)
        both = tile_dot(x, jnp.concatenate([x, left], axis=1))
        right = tile_dot(y, y)
        products[t, 0] = both[:, K:]
        products[t, 1] = jnp.where(row_at <= col_at, both[:, :K], right)
        diagonal = jnp.sum(jnp.where(row_at == col_at, right, 0.0), axis=0, keepdims=True)
        diagonals[t] = jnp.broadcast_to(diagonal, (8, K))

    here = lax.axis_index("col")
    firsts = [(first_kept, 0), (first_sent, 0), (first_sent, 1), (first_kept, 1)]
    seconds = [(second_kept, 0), (second_kept, 1), (second_sent, 1), (second_sent, 0)]
    for away in range(COLS):
        column = here ^ away
        start = pl.multiple_of(column * PART, PART)
        along, across = away // 2, away % 2
        for low, (ref, at) in ((0, firsts[along]), (TILES // 2, seconds[along])):
            for n in range(TILES):
                ref[at, across, n * PART : (n + 1) * PART, :] = products[
                    low + n // 2, n % 2, pl.ds(start, PART), :
                ]
        ref, at = firsts[along]
        ref[at, across, EARLY:, :] = diagonals[column]
        ref, at = seconds[along]
        ref[at, across, EARLY:, :] = gram[pl.ds(start, PART), :]


def late_kernel(
    got_ref, right_ref, y_ref, out_ref, rows, ends
):
    for pair in range(HOLDERS // 2):
        part = got_ref[16 * pair : 16 * pair + 16, :].astype(jnp.float32)
        for side in range(2):
            holder = 2 * pair + side
            mine = part[8 * side : 8 * side + 8]
            for which in range(2):
                for q in range(EACH):
                    at = 8 * (which * SLICED + holder * EACH + q)
                    from_lane = (which * EACH + q) * K
                    rows[at : at + 8, :] = mine[:, from_lane : from_lane + K]
            ends[8 * holder : 8 * holder + 8, :] = mine[:, LAST * K :]
    right = right_ref[...]
    filler = jnp.zeros((LONG - S, K), jnp.bfloat16)

    def panel_tile(t, which):
        body = rows[pl.ds(8 * which * SLICED + t, SLICED, stride=8), :]
        end = ends[pl.ds(8 * which * SHARED + t, SHARED, stride=8), :]
        return jnp.concatenate(
            [body.astype(jnp.bfloat16), end.astype(jnp.bfloat16), filler], axis=0
        )

    for t in range(TILES):
        core = plain_dot(right, panel_tile(t, 1))
        part_right = plain_dot(y_ref[t], panel_tile(t, 0))
        for c in range(COLS):
            base = 2 * t * PART
            out_ref[c, base : base + PART, :] = core[c * PART : (c + 1) * PART]
            out_ref[c, base + PART : base + 2 * PART, :] = part_right[c * PART : (c + 1) * PART]


def route_kernel(owner_ref, kept_ref, came_ref, late_ref, out_ref, sums):
    for t in range(TILES):
        base = 2 * t * PART
        sums[t, : 2 * PART, :] = kept_ref[EARLY_AT[t], :] + came_ref[EARLY_AT[t], :]
        total = late_ref[0, base : base + 2 * PART, :]
        for c in range(1, COLS):
            total = total + late_ref[c, base : base + 2 * PART, :]
        sums[t, 2 * PART :, :] = total
    diagonal = kept_ref[EARLY:FIRST, :] + came_ref[EARLY:FIRST, :]
    gram = kept_ref[FIRST + EARLY :, :] + came_ref[FIRST + EARLY :, :]
    for column in range(COLS):
        for place, t in enumerate(owned_tiles(owner_ref, column)):
            there = slice(4 * place * PART, 4 * (place + 1) * PART)

            @pl.when(t >= 0)
            def _():
                out_ref[column, there, :] = sums[t]

            @pl.when(t < 0)
            def _():
                out_ref[column, there, :] = jnp.zeros((4 * PART, K), jnp.float32)

        out_ref[column, 8 * PART : 9 * PART, :] = gram
        out_ref[column, 9 * PART :, :] = jnp.zeros((8, K), jnp.float32)

    here = lax.axis_index("col")
    place = jnp.int32(0)
    for t in range(TILES):
        place = place + ((t < here) & (owner_ref[t] == owner_ref[here])).astype(jnp.int32)
    row_at = lax.broadcasted_iota(jnp.int32, (8, K), 0)
    out_ref[owner_ref[here], 9 * PART :, :] = jnp.where(row_at == place, diagonal, 0.0)


def final_kernel(got_ref, lo_ref, lc_ref, ln_ref, ro_ref, rc_ref):
    row_at = lax.broadcasted_iota(jnp.int32, (K, K), 0)
    col_at = lax.broadcasted_iota(jnp.int32, (K, K), 1)

    def whole(at):
        return jnp.concatenate(
            [got_ref[c, at * PART : (at + 1) * PART, :] for c in range(COLS)], axis=0
        )

    gram = whole(8)
    diagonals = got_ref[0, 9 * PART :, :]
    for c in range(1, COLS):
        diagonals = diagonals + got_ref[c, 9 * PART :, :]
    for place in range(2):
        part_left = whole(4 * place)
        mixed = whole(4 * place + 1)
        core = whole(4 * place + 2)
        part_right = whole(4 * place + 3)
        diagonal = diagonals[place : place + 1]
        across = mixed.T
        lo_ref[place] = jnp.where(row_at <= col_at, mixed, across)
        ro_ref[place] = jnp.where(
            row_at > col_at, mixed, jnp.where(row_at < col_at, across, diagonal)
        )
        rc_ref[place] = -part_right
        lc_ref[place] = exact_dot(part_left, core)
        ln_ref[place] = exact_dot(core, exact_dot(gram, core), 0)


def swapped(block, away):
    return lax.ppermute(block, "col", [(c, c ^ away) for c in range(COLS)])


def cost(micros):
    return pl.CostEstimate(flops=micros * 1000000000, bytes_accessed=0, transcendentals=0)


def smem(count):
    return [pl.BlockSpec(memory_space=pltpu.SMEM)] * count


def vmem(count):
    return [pl.BlockSpec(memory_space=pltpu.VMEM)] * count


def per_device(panel_u, panel_v, panel_rank, trail_x, trail_y, trail_rank, tile_cols, owner):
    params = pltpu.CompilerParams(vmem_limit_bytes=VMEM)
    xt = jnp.swapaxes(trail_x, 1, 2)
    yt = jnp.swapaxes(trail_y, 1, 2)
    ut = jnp.swapaxes(panel_u, 1, 2)[0]
    vt = jnp.swapaxes(panel_v, 1, 2)[0]
    owners = owner[:, 0]

    with jax.named_scope("slices_out"):
        wanted = jnp.pad(tile_cols.astype(jnp.bfloat16), (0, K - TILES))
        kept = jnp.concatenate(
            [
                keep(ut, panel_rank[0]),
                keep(vt, panel_rank[0]),
                jnp.broadcast_to(wanted, (16, K)),
            ]
        )
        slices = pl.pallas_call(
            slices_kernel,
            in_specs=vmem(1),
            out_shape=jax.ShapeDtypeStruct((PEERS * BLOCK, K), jnp.bfloat16),
            scratch_shapes=[
                pltpu.VMEM((2 * SLICED + SPARE, K), jnp.float32),
                pltpu.VMEM((2 * SHARED, K), jnp.float32),
                pltpu.VMEM((PEERS * BLOCK + 4 * SPARE, K), jnp.float32),
            ],
            compiler_params=params,
            cost_estimate=cost(1),
            name="slices_out",
        )(kept)
        held = lax.all_to_all(slices.reshape(PEERS, BLOCK, K), "row", 0, 0)
        held = held.reshape(PEERS, BLOCK * K)

    with jax.named_scope("first_products"):
        first = jax.ShapeDtypeStruct((2, 2, FIRST, K), jnp.float32)
        second = jax.ShapeDtypeStruct((2, 2, SECOND, K), jnp.float32)
        *pieces, right_turned, y_turned = pl.pallas_call(
            early_kernel,
            in_specs=smem(2) + vmem(3),
            out_shape=[
                first,
                first,
                second,
                second,
                jax.ShapeDtypeStruct((K, LONG), jnp.bfloat16),
                jax.ShapeDtypeStruct((TILES, K, LONG), jnp.bfloat16),
            ],
            scratch_shapes=[
                pltpu.VMEM((TILES, 2, K, K), jnp.float32),
                pltpu.VMEM((TILES, 8, K), jnp.float32),
                pltpu.VMEM((K, K), jnp.float32),
            ],
            compiler_params=params,
            cost_estimate=cost(4),
            name="first_products",
        )(owners, trail_rank, kept, xt, yt)

    held, *_ = lax.optimization_barrier((held, *pieces))

    with jax.named_scope("first_sum"):
        first_sent, first_kept, second_sent, second_kept = pieces
        first = first_kept + swapped(first_sent, 2)
        second = second_kept + swapped(second_sent, 6)
        first = first[0] + swapped(first[1], 6)
        second = second[0] + swapped(second[1], 2)
        early_kept = jnp.concatenate([first[0], second[0]])
        early_came = swapped(jnp.concatenate([first[1], second[1]]), 1)

    with jax.named_scope("tiles_asked_for"):
        asked = held[:, WIDE : WIDE + TILES].reshape(HOLDERS, 2, TILES)
        asked = jnp.where(lax.axis_index("row") % 2 == 0, asked[:, 0], asked[:, 1])
        chosen = asked.astype(jnp.int32).reshape(HOLDERS * TILES, 1) == lax.broadcasted_iota(
            jnp.int32, (HOLDERS * TILES, PEERS), 1
        )
        sent = jnp.dot(
            chosen.astype(jnp.bfloat16), held[:, :WIDE], preferred_element_type=jnp.float32
        ).astype(jnp.bfloat16)
        same_core = [list(range(core, PEERS, 2)) for core in range(2)]
        got = lax.all_to_all(
            sent.reshape(HOLDERS, TILES, WIDE), "row", 0, 0, axis_index_groups=same_core
        )
        got, early_kept, early_came, owners = lax.optimization_barrier(
            (got, early_kept, early_came, owners)
        )

    with jax.named_scope("second_products"):
        late = pl.pallas_call(
            late_kernel,
            in_specs=vmem(3),
            out_shape=jax.ShapeDtypeStruct((COLS, 2 * K, K), jnp.float32),
            scratch_shapes=[
                pltpu.VMEM((2 * SLICED * TILES + SPARE, K), jnp.float32),
                pltpu.VMEM((HOLDERS * TILES + SPARE, K), jnp.float32),
            ],
            compiler_params=params,
            cost_estimate=cost(4),
            name="second_products",
        )(got.reshape(HOLDERS * TILES, WIDE), right_turned, y_turned)
        late = lax.all_to_all(late, "col", 0, 0)

    with jax.named_scope("parts_to_owners"):
        owned = pl.pallas_call(
            route_kernel,
            in_specs=smem(1) + vmem(3),
            out_shape=jax.ShapeDtypeStruct((COLS, OWNED, K), jnp.float32),
            scratch_shapes=[pltpu.VMEM((TILES, 4 * PART, K), jnp.float32)],
            compiler_params=params,
            cost_estimate=cost(1),
            name="parts_to_owners",
        )(owners, early_kept, early_came, late)
        owned = lax.all_to_all(owned, "col", 0, 0)

    with jax.named_scope("owned_results"):
        result = jax.ShapeDtypeStruct((2, K, K), jnp.float32)
        return pl.pallas_call(
            final_kernel,
            out_shape=(result,) * 5,
            compiler_params=params,
            name="owned_results",
        )(owned)


def solution(mesh):
    placed = (
        P("row", None, "col"),
        P("row", None, "col"),
        P("row"),
        P("row", None, "col"),
        P("row", None, "col"),
        P("row"),
        P("row"),
        P("row", None),
    )
    return jax.shard_map(
        per_device,
        mesh=mesh,
        in_specs=placed,
        out_specs=(P(("row", "col"), None, None),) * 5,
        check_vma=False,
    )
```

```python
import jax
import jax.numpy as jnp
from jax import lax
from jax.experimental import pallas as pl
from jax.experimental.pallas import tpu as pltpu
from jax.sharding import PartitionSpec as P

K = 128
S = 336
TILES = 8
PEERS = 64
COLS = 8
HOLDERS = PEERS // 2
EACH = 10
SLICED = EACH * HOLDERS
SHARED = S - SLICED
LAST = 2 * EACH
WIDE = (LAST + 1) * K
BLOCK = 24
LONG = 3 * K
RUNS = [(0, 4), (4, 8), (8, 12), (12, 16), (16, 21)]
PART = K // COLS
EARLY = TILES * PART
FIRST = EARLY + 8
SECOND = EARLY + PART
OWNED = 8 * PART + PART + 8
EARLY_AT = [
    slice(at, at + 2 * PART)
    for base in (0, FIRST)
    for at in range(base, base + EARLY, 2 * PART)
]
SPARE = 16
VMEM = 32 * 1024 * 1024


def tile_dot(first, second):
    return lax.dot_general(
        first, second, (((0,), (0,)), ((), ())), preferred_element_type=jnp.float32
    )


def plain_dot(first, second):
    return jnp.dot(first, second, preferred_element_type=jnp.float32)


def exact_dot(first, second, lhs_dim=1):
    return lax.dot_general(
        first,
        second,
        (((lhs_dim,), (0,)), ((), ())),
        precision=lax.Precision.HIGHEST,
        preferred_element_type=jnp.float32,
    )


def keep(block, rank):
    lane = lax.broadcasted_iota(jnp.int32, block.shape, block.ndim - 1)
    return jnp.where(lane < rank, block, jnp.zeros_like(block))


def owned_tiles(owner_ref, column):
    first = jnp.int32(-1)
    second = jnp.int32(-1)
    for t in range(TILES):
        mine = owner_ref[t] == column
        second = jnp.where(mine & (first >= 0), t, second)
        first = jnp.where(mine & (first < 0), t, first)
    return first, second


def slices_kernel(kept_ref, slices_ref, rows, ends, blocks):
    wanted = kept_ref[2 * S : 2 * S + 16, :].astype(jnp.float32)
    wanted = jnp.concatenate([wanted, wanted], axis=0)
    for which in range(2):
        kept = kept_ref[which * S : (which + 1) * S, :]
        rows[which * SLICED : (which + 1) * SLICED, :] = kept[:SLICED].astype(jnp.float32)
        ends[which * SHARED : (which + 1) * SHARED, :] = kept[SLICED:].astype(jnp.float32)
    for core in range(2):

        def place(at, part):
            blocks[pl.ds(core * BLOCK + at, HOLDERS, stride=2 * BLOCK), :] = part

        for which in range(2):
            for q in range(EACH):
                place(which * EACH + q, rows[pl.ds(which * SLICED + q, HOLDERS, stride=EACH), :])
        place(LAST, ends[...])
        place(LAST + 1, wanted)
        for at in range(LAST + 2, BLOCK):
            place(at, jnp.zeros((HOLDERS, K), jnp.float32))
    slices_ref[...] = blocks[: PEERS * BLOCK, :].astype(jnp.bfloat16)


def turned(block):
    filler = jnp.zeros((LONG - S, K), block.dtype)
    return jnp.concatenate([block, filler], axis=0).T


def early_kernel(
    owner_ref,
    rank_ref,
    kept_ref,
    x_ref,
    y_ref,
    first_sent,
    first_kept,
    second_sent,
    second_kept,
    right_turned,
    y_turned,
    products,
    diagonals,
    gram,
):
    left = kept_ref[:S]
    right_turned[...] = turned(kept_ref[S : 2 * S])
    gram[...] = tile_dot(left, left)
    row_at = lax.broadcasted_iota(jnp.int32, (K, K), 0)
    col_at = lax.broadcasted_iota(jnp.int32, (K, K), 1)
    for t in range(TILES):
        x = keep(x_ref[t], rank_ref[t])
        y = keep(y_ref[t], rank_ref[t])
        y_turned[t] = turned(y)
        both = tile_dot(x, jnp.concatenate([x, left], axis=1))
        right = tile_dot(y, y)
        products[t, 0] = both[:, K:]
        products[t, 1] = jnp.where(row_at <= col_at, both[:, :K], right)
        diagonal = jnp.sum(jnp.where(row_at == col_at, right, 0.0), axis=0, keepdims=True)
        diagonals[t] = jnp.broadcast_to(diagonal, (8, K))

    here = lax.axis_index("col")
    firsts = [(first_kept, 0), (first_sent, 0), (first_sent, 1), (first_kept, 1)]
    seconds = [(second_kept, 0), (second_kept, 1), (second_sent, 1), (second_sent, 0)]
    for away in range(COLS):
        column = here ^ away
        start = pl.multiple_of(column * PART, PART)
        along, across = away // 2, away % 2
        for low, (ref, at) in ((0, firsts[along]), (TILES // 2, seconds[along])):
            for n in range(TILES):
                ref[at, across, n * PART : (n + 1) * PART, :] = products[
                    low + n // 2, n % 2, pl.ds(start, PART), :
                ]
        ref, at = firsts[along]
        ref[at, across, EARLY:, :] = diagonals[column]
        ref, at = seconds[along]
        ref[at, across, EARLY:, :] = gram[pl.ds(start, PART), :]


def gather_kernel(held_ref, out_ref, blocks, sent, gone):
    blocks[: PEERS * BLOCK, :] = held_ref[...].astype(jnp.float32)
    asked = jnp.where(
        lax.axis_index("row") % 2 == 0,
        blocks[pl.ds(LAST + 1, HOLDERS, stride=2 * BLOCK), :],
        blocks[pl.ds(LAST + 1 + BLOCK, HOLDERS, stride=2 * BLOCK), :],
    )
    count = HOLDERS * TILES
    holder = lax.broadcasted_iota(jnp.int32, (count, HOLDERS), 1)
    spread = lax.broadcasted_iota(jnp.int32, (count, HOLDERS), 0) // TILES == holder
    asked = plain_dot(spread.astype(jnp.bfloat16), asked.astype(jnp.bfloat16))
    tile = lax.broadcasted_iota(jnp.int32, (count, K), 0) % TILES
    lane = lax.broadcasted_iota(jnp.int32, (count, K), 1)
    asked = jnp.sum(jnp.where(lane == tile, asked, 0.0), axis=1, keepdims=True)
    peer = lax.broadcasted_iota(jnp.int32, (count, PEERS), 1)
    chosen = (asked.astype(jnp.int32) == peer).astype(jnp.bfloat16)
    copies = []
    for run, (start, stop) in enumerate(RUNS):
        parts = [
            blocks[pl.ds(at, PEERS, stride=BLOCK), :].astype(jnp.bfloat16)
            for at in range(start, stop)
        ]
        lanes = slice(start * K, stop * K)
        sent[:, lanes] = plain_dot(chosen, jnp.concatenate(parts, axis=1)).astype(jnp.bfloat16)
        copy = pltpu.make_async_copy(sent.at[:, lanes], out_ref.at[:, lanes], gone.at[run])
        copy.start()
        copies.append(copy)
    for copy in copies:
        copy.wait()


def late_kernel(
    got_ref, right_ref, y_ref, out_ref, rows, ends
):
    for pair in range(HOLDERS // 2):
        part = got_ref[16 * pair : 16 * pair + 16, :].astype(jnp.float32)
        for side in range(2):
            holder = 2 * pair + side
            mine = part[8 * side : 8 * side + 8]
            for which in range(2):
                for q in range(EACH):
                    at = 8 * (which * SLICED + holder * EACH + q)
                    from_lane = (which * EACH + q) * K
                    rows[at : at + 8, :] = mine[:, from_lane : from_lane + K]
            ends[8 * holder : 8 * holder + 8, :] = mine[:, LAST * K :]
    right = right_ref[...]
    filler = jnp.zeros((LONG - S, K), jnp.bfloat16)

    def panel_tile(t, which):
        body = rows[pl.ds(8 * which * SLICED + t, SLICED, stride=8), :]
        end = ends[pl.ds(8 * which * SHARED + t, SHARED, stride=8), :]
        return jnp.concatenate(
            [body.astype(jnp.bfloat16), end.astype(jnp.bfloat16), filler], axis=0
        )

    for t in range(TILES):
        core = plain_dot(right, panel_tile(t, 1))
        part_right = plain_dot(y_ref[t], panel_tile(t, 0))
        for c in range(COLS):
            base = 2 * t * PART
            out_ref[c, base : base + PART, :] = core[c * PART : (c + 1) * PART]
            out_ref[c, base + PART : base + 2 * PART, :] = part_right[c * PART : (c + 1) * PART]


def route_kernel(owner_ref, early_ref, late_ref, out_ref, sums):
    for t in range(TILES):
        base = 2 * t * PART
        sums[t, : 2 * PART, :] = early_ref[EARLY_AT[t], :]
        total = late_ref[0, base : base + 2 * PART, :]
        for c in range(1, COLS):
            total = total + late_ref[c, base : base + 2 * PART, :]
        sums[t, 2 * PART :, :] = total
    diagonal = early_ref[EARLY:FIRST, :]
    gram = early_ref[FIRST + EARLY :, :]
    for column in range(COLS):
        for place, t in enumerate(owned_tiles(owner_ref, column)):
            there = slice(4 * place * PART, 4 * (place + 1) * PART)

            @pl.when(t >= 0)
            def _():
                out_ref[column, there, :] = sums[t]

            @pl.when(t < 0)
            def _():
                out_ref[column, there, :] = jnp.zeros((4 * PART, K), jnp.float32)

        out_ref[column, 8 * PART : 9 * PART, :] = gram
        out_ref[column, 9 * PART :, :] = jnp.zeros((8, K), jnp.float32)

    here = lax.axis_index("col")
    place = jnp.int32(0)
    for t in range(TILES):
        place = place + ((t < here) & (owner_ref[t] == owner_ref[here])).astype(jnp.int32)
    row_at = lax.broadcasted_iota(jnp.int32, (8, K), 0)
    out_ref[owner_ref[here], 9 * PART :, :] = jnp.where(row_at == place, diagonal, 0.0)


def final_kernel(got_ref, lo_ref, lc_ref, ln_ref, ro_ref, rc_ref):
    row_at = lax.broadcasted_iota(jnp.int32, (K, K), 0)
    col_at = lax.broadcasted_iota(jnp.int32, (K, K), 1)

    def whole(at):
        return jnp.concatenate(
            [got_ref[c, at * PART : (at + 1) * PART, :] for c in range(COLS)], axis=0
        )

    gram = whole(8)
    diagonals = got_ref[0, 9 * PART :, :]
    for c in range(1, COLS):
        diagonals = diagonals + got_ref[c, 9 * PART :, :]
    for place in range(2):
        part_left = whole(4 * place)
        mixed = whole(4 * place + 1)
        core = whole(4 * place + 2)
        part_right = whole(4 * place + 3)
        diagonal = diagonals[place : place + 1]
        across = mixed.T
        lo_ref[place] = jnp.where(row_at <= col_at, mixed, across)
        ro_ref[place] = jnp.where(
            row_at > col_at, mixed, jnp.where(row_at < col_at, across, diagonal)
        )
        rc_ref[place] = -part_right
        lc_ref[place] = exact_dot(part_left, core)
        ln_ref[place] = exact_dot(core, exact_dot(gram, core), 0)


def swapped(block, away):
    return lax.ppermute(block, "col", [(c, c ^ away) for c in range(COLS)])


def cost(micros):
    return pl.CostEstimate(flops=micros * 1000000000, bytes_accessed=0, transcendentals=0)


def smem(count):
    return [pl.BlockSpec(memory_space=pltpu.SMEM)] * count


def vmem(count):
    return [pl.BlockSpec(memory_space=pltpu.VMEM)] * count


def per_device(panel_u, panel_v, panel_rank, trail_x, trail_y, trail_rank, tile_cols, owner):
    params = pltpu.CompilerParams(vmem_limit_bytes=VMEM)
    xt = jnp.swapaxes(trail_x, 1, 2)
    yt = jnp.swapaxes(trail_y, 1, 2)
    ut = jnp.swapaxes(panel_u, 1, 2)[0]
    vt = jnp.swapaxes(panel_v, 1, 2)[0]
    owners = owner[:, 0]

    with jax.named_scope("slices_out"):
        wanted = jnp.pad(tile_cols.astype(jnp.bfloat16), (0, K - TILES))
        kept = jnp.concatenate(
            [
                keep(ut, panel_rank[0]),
                keep(vt, panel_rank[0]),
                jnp.broadcast_to(wanted, (16, K)),
            ]
        )
        slices = pl.pallas_call(
            slices_kernel,
            in_specs=vmem(1),
            out_shape=jax.ShapeDtypeStruct((PEERS * BLOCK, K), jnp.bfloat16),
            scratch_shapes=[
                pltpu.VMEM((2 * SLICED + SPARE, K), jnp.float32),
                pltpu.VMEM((2 * SHARED, K), jnp.float32),
                pltpu.VMEM((PEERS * BLOCK + 4 * SPARE, K), jnp.float32),
            ],
            compiler_params=params,
            cost_estimate=cost(1),
            name="slices_out",
        )(kept)
        held = lax.all_to_all(slices.reshape(PEERS, BLOCK, K), "row", 0, 0)
        held = held.reshape(PEERS * BLOCK, K)

    with jax.named_scope("first_products"):
        first = jax.ShapeDtypeStruct((2, 2, FIRST, K), jnp.float32)
        second = jax.ShapeDtypeStruct((2, 2, SECOND, K), jnp.float32)
        *pieces, right_turned, y_turned = pl.pallas_call(
            early_kernel,
            in_specs=smem(2) + vmem(3),
            out_shape=[
                first,
                first,
                second,
                second,
                jax.ShapeDtypeStruct((K, LONG), jnp.bfloat16),
                jax.ShapeDtypeStruct((TILES, K, LONG), jnp.bfloat16),
            ],
            scratch_shapes=[
                pltpu.VMEM((TILES, 2, K, K), jnp.float32),
                pltpu.VMEM((TILES, 8, K), jnp.float32),
                pltpu.VMEM((K, K), jnp.float32),
            ],
            compiler_params=params,
            cost_estimate=cost(4),
            name="first_products",
        )(owners, trail_rank, kept, xt, yt)

    held, *_ = lax.optimization_barrier((held, *pieces))

    with jax.named_scope("first_sum"):
        first_sent, first_kept, second_sent, second_kept = pieces
        first = first_kept + swapped(first_sent, 2)
        second = second_kept + swapped(second_sent, 6)
        first = first[0] + swapped(first[1], 6)
        second = second[0] + swapped(second[1], 2)
        early_kept = jnp.concatenate([first[0], second[0]])
        early_came = swapped(jnp.concatenate([first[1], second[1]]), 1)

    with jax.named_scope("tiles_asked_for"):
        sent = pl.pallas_call(
            gather_kernel,
            in_specs=vmem(1),
            out_specs=pl.BlockSpec(memory_space=pl.ANY),
            out_shape=jax.ShapeDtypeStruct((HOLDERS * TILES, WIDE), jnp.bfloat16),
            scratch_shapes=[
                pltpu.VMEM((PEERS * BLOCK + 4 * SPARE, K), jnp.float32),
                pltpu.VMEM((HOLDERS * TILES, WIDE), jnp.bfloat16),
                pltpu.SemaphoreType.DMA((len(RUNS),)),
            ],
            compiler_params=params,
            cost_estimate=cost(1),
            name="tiles_asked_for",
        )(held)
        same_core = [list(range(core, PEERS, 2)) for core in range(2)]
        got = lax.all_to_all(
            sent.reshape(HOLDERS, TILES, WIDE), "row", 0, 0, axis_index_groups=same_core
        )
        got, early, owners = lax.optimization_barrier((got, early_kept + early_came, owners))

    with jax.named_scope("second_products"):
        late = pl.pallas_call(
            late_kernel,
            in_specs=vmem(3),
            out_shape=jax.ShapeDtypeStruct((COLS, 2 * K, K), jnp.float32),
            scratch_shapes=[
                pltpu.VMEM((2 * SLICED * TILES + SPARE, K), jnp.float32),
                pltpu.VMEM((HOLDERS * TILES + SPARE, K), jnp.float32),
            ],
            compiler_params=params,
            cost_estimate=cost(4),
            name="second_products",
        )(got.reshape(HOLDERS * TILES, WIDE), right_turned, y_turned)
        late = lax.all_to_all(late, "col", 0, 0)

    with jax.named_scope("parts_to_owners"):
        owned = pl.pallas_call(
            route_kernel,
            in_specs=smem(1) + vmem(2),
            out_shape=jax.ShapeDtypeStruct((COLS, OWNED, K), jnp.float32),
            scratch_shapes=[pltpu.VMEM((TILES, 4 * PART, K), jnp.float32)],
            compiler_params=params,
            cost_estimate=cost(1),
            name="parts_to_owners",
        )(owners, early, late)
        owned = lax.all_to_all(owned, "col", 0, 0)

    with jax.named_scope("owned_results"):
        result = jax.ShapeDtypeStruct((2, K, K), jnp.float32)
        return pl.pallas_call(
            final_kernel,
            out_shape=(result,) * 5,
            compiler_params=params,
            name="owned_results",
        )(owned)


def solution(mesh):
    placed = (
        P("row", None, "col"),
        P("row", None, "col"),
        P("row"),
        P("row", None, "col"),
        P("row", None, "col"),
        P("row"),
        P("row"),
        P("row", None),
    )
    return jax.shard_map(
        per_device,
        mesh=mesh,
        in_specs=placed,
        out_specs=(P(("row", "col"), None, None),) * 5,
        check_vma=False,
    )
```
